32 devices in a mesh: scen: 2 (over y), region: 4 (over z), dest: 4 (over x, core).
Axes of the slice: x: 2, y: 2, z: 4, core: 2. Of those that a mesh axis runs over, the one named last changes fastest.
Arguments:
- density: float32 [8, 1024, 1024], P(None, ('scen', 'region'), 'dest'), parts along dimension 1, may hold values from 0.01 to 1.5, as said below
- anchor: float32 [1024, 1024], P(('scen', 'region'), 'dest'), parts along dimension 0, may hold values from 0.005 to 0.3
- feeds: int32 [512, 4], P('region'), may hold values from -1 to 511, as said below
- turns: int32 [512, 4], P('region'), may hold values from 1 to 8
- plan: int32 [3, 512], P(None, 'region'), may hold values from 0 to 7
- capacity_levels: float32 [8], replicated, may hold values from 0.2 to 0.8
Outputs:
- final_density: float32 [8, 1024, 1024], P(None, ('scen', 'region'), 'dest'), parts along dimension 1
The draws below stay inside these ranges and needn't reach their ends.
There are 2 independent parts, one for each index of `scen`. The reference program is written for one: setup_inputs(seed, part) draws one part's arguments, and reference() takes and returns one part's arrays. A program takes and returns all parts, laid end to end along the dimension named above; an argument that names none is the same for every part. Nothing has to cross between parts.
Inputs may be any that keep to these rules, and one draw needn't show every extreme that they name: Each per-commodity density is positive. `feeds`: -1 marks an unused entry. The lists of one device's links hold at most 64 entries naming links of any one other device, and name at most 32 distinct links of it; every device reaches both bounds for some other device.
All inputs are finite; a program needn't handle non-finite values.
Results may differ from the reference program's by a relative error of at most 0.0001.
Values sent between devices are 32-bit elements; how exact they have to be, the bound alone decides.
A program may use at most 64 MiB of HBM per device.

```python
import math
import jax
import jax.numpy as jnp

COMM = 1024
LINK_DEV = 128
CELLS = 8
STEPS = 3
LEVELS = 8
LINKS = 512
CAP = 32
N_REGION = 4


def commodity_ramp():
    return 0.5 + jnp.arange(COMM, dtype=jnp.float32) / COMM


def draw_density(key, part):
    key = jax.random.fold_in(key, 1)
    first_key = jax.random.fold_in(key, 0)
    values = jnp.exp(jax.random.uniform(first_key, (CELLS, LINKS, COMM), jnp.float32, jnp.log(0.1), 0.0))
    return (values * commodity_ramp()).astype(jnp.float32)


def draw_anchor(key, part):
    key = jax.random.fold_in(key, 2)
    first_key = jax.random.fold_in(key, 0)
    values = jnp.exp(jax.random.uniform(first_key, (LINKS, COMM), jnp.float32, jnp.log(0.02), jnp.log(0.2)))
    return (values * commodity_ramp()).astype(jnp.float32)


def draw_feeds(key, part):
    key = jax.random.fold_in(key, 3)
    degree_key, order_key, pick_key, spread_key = jax.random.split(key, 4)
    entries = 2 * LINK_DEV
    junctions = LINK_DEV // 2
    spread = LINK_DEV // 2
    others = entries - CAP
    regions = jnp.arange(N_REGION, dtype=jnp.int32)[:, None]
    degree = jax.random.randint(degree_key, (N_REGION, junctions), 1, 5)
    degree = jnp.where(jnp.arange(junctions)[None, :] < CAP // 4, 4, degree)
    slot_in = jnp.arange(entries, dtype=jnp.int32)[None, :] % 4
    is_live = slot_in < jnp.repeat(degree, 4, axis=1)
    order_keys = jax.random.split(order_key, N_REGION)
    placing = jax.vmap(lambda sub_key: jax.random.permutation(sub_key, others))(order_keys).astype(jnp.int32)
    pick_keys = jax.random.split(pick_key, N_REGION)
    forced_local = jax.vmap(lambda sub_key: jax.random.permutation(sub_key, LINK_DEV)[:CAP])(pick_keys).astype(jnp.int32)
    spread_owner = jnp.where(placing < spread, (regions + 2 + placing % (N_REGION - 2)) % N_REGION, regions)
    forced_owner = jnp.broadcast_to((regions + 1) % N_REGION, (N_REGION, CAP))
    owners = jnp.concatenate([forced_owner, spread_owner], axis=1)
    spread_local = jax.random.randint(spread_key, (N_REGION, others), 0, LINK_DEV).astype(jnp.int32)
    local_ids = jnp.concatenate([forced_local, spread_local], axis=1)
    named_links = jnp.where(is_live, owners * LINK_DEV + local_ids, -1)
    named_links = jnp.repeat(named_links.reshape(N_REGION, junctions, 4), 2, axis=1)
    return named_links.reshape(LINKS, 4).astype(jnp.int32)


def set_ends(values, rng, low, top_value):
    index_at = [jax.random.randint(jax.random.fold_in(rng, axis), (), 0, length) for axis, length in enumerate(values.shape)]
    widest = values.shape.index(max(values.shape))
    beside = index_at[:widest] + [(index_at[widest] + 1) % values.shape[widest]] + index_at[widest + 1:]
    return values.at[tuple(index_at)].set(low).at[tuple(beside)].set(top_value)


def setup_inputs(seed: int = 0, part: int = 0) -> dict:
    splits = jax.random.split(jax.random.key(seed), 7)
    part_keys = jax.random.split(jax.random.fold_in(splits[6], part), 7)
    return {
        "density": draw_density(jax.random.fold_in(jax.random.fold_in(splits[6], part), 71), part),
        "anchor": draw_anchor(jax.random.fold_in(jax.random.fold_in(splits[6], part), 71), part),
        "feeds": draw_feeds(jax.random.fold_in(splits[6], 71), part),
        "turns": set_ends(jax.random.randint(splits[3], (LINKS, 4), 1, 9), jax.random.fold_in(splits[3], 1), 1, 8).astype(jnp.int32),
        "plan": set_ends(jax.random.randint(splits[4], (STEPS, LINKS), 0, LEVELS), jax.random.fold_in(splits[4], 1), 0, LEVELS - 1).astype(jnp.int32),
        "capacity_levels": jnp.clip(jnp.exp(jax.random.uniform(splits[5], (LEVELS,), jnp.float32, math.log(0.2), math.log(0.8))), 0.2, 0.8),
    }


FREE_SPEED = 0.8
WAVE_SPEED = 0.4
JAM_FACTOR = 2.0
EXIT_WEIGHT = 4.0


def reference(density, anchor, feeds, turns, plan, capacity_levels):
    num_cells, num_links, commodity_width = density.shape
    block_span = min(128, commodity_width)
    flat_feed = feeds.reshape(-1)
    is_live = flat_feed >= 0
    target_rows = jnp.where(is_live, flat_feed, num_links).astype(jnp.int32)
    source_rows = jnp.where(is_live, flat_feed, 0).astype(jnp.int32)
    live_turn = jnp.where(is_live, turns.reshape(-1), 0).astype(jnp.int32)
    count_total = jax.ops.segment_sum(live_turn, target_rows, num_segments=num_links + 1)[:num_links]
    denominator = count_total.astype(jnp.float32) + EXIT_WEIGHT
    turn_weight = live_turn.astype(jnp.float32)
    anchor_total = jnp.sum(anchor, axis=1)
    level_ids = jnp.arange(capacity_levels.shape[0], dtype=jnp.int32)
    for step_index in range(STEPS):
        cell_sum = jnp.sum(density, axis=2)
        level_match = plan[step_index][:, None] == level_ids[None, :]
        capacity_now = jnp.sum(jnp.where(level_match, capacity_levels[None, :], jnp.float32(0.0)), axis=1) * COMM
        sending = jnp.minimum(FREE_SPEED * cell_sum, capacity_now[None, :])
        receiving = jnp.minimum(capacity_now[None, :], WAVE_SPEED * (JAM_FACTOR * COMM - cell_sum))
        per_count = sending[num_cells - 1] / denominator
        unit_share = per_count / cell_sum[num_cells - 1]
        demand = jnp.sum((turn_weight * per_count[source_rows]).reshape(num_links, 4), axis=1) + anchor_total
        ratio = receiving[0] / jnp.maximum(receiving[0], demand)
        mixing = (turn_weight * unit_share[source_rows]).reshape(num_links, 4)
        granted = (turn_weight.reshape(num_links, 4) * ratio[:, None]).reshape(-1)
        passed = jax.ops.segment_sum(granted, target_rows, num_segments=num_links + 1)[:num_links]
        last_rows = density[num_cells - 1]
        pieces = []
        for block_start in range(0, commodity_width, block_span):
            block_rows = last_rows[:, block_start:block_start + block_span]
            picked = block_rows[source_rows].reshape(num_links, 4, block_rows.shape[1])
            gathered = jnp.sum(mixing[:, :, None] * picked, axis=1)
            pieces.append(ratio[:, None] * (gathered + anchor[:, block_start:block_start + block_span]))
        inflow = jnp.concatenate(pieces, axis=1)
        outflow = (unit_share * (passed + EXIT_WEIGHT))[:, None] * last_rows
        through = jnp.minimum(sending[:-1], receiving[1:])
        moving = (through / cell_sum[:-1])[:, :, None] * density[:-1]
        density = density - jnp.pad(moving, ((0, 1), (0, 0), (0, 0))) + jnp.pad(moving, ((1, 0), (0, 0), (0, 0)))
        density = density.at[num_cells - 1].add(-outflow).at[0].add(inflow)
    return density
```

```python
import functools

import jax
import jax.numpy as jnp
from jax import lax
from jax.experimental import pallas as pl
from jax.experimental.pallas import tpu as pltpu
from jax.sharding import PartitionSpec as P

COMM = 1024


FREE_SPEED = 0.8
WAVE_SPEED = 0.4
JAM_FACTOR = 2.0
EXIT_WEIGHT = 4.0


def one_hot_table(positions, segments):
    return positions[:, None] == jnp.arange(segments, dtype=jnp.int32)[None, :]


def table_total(values, table):
    return jnp.sum(jnp.where(table, values[:, None], 0), axis=0)


def slot_ranks(chosen, owners, peers):
    member = chosen[:, None] & (owners[:, None] == jnp.arange(peers, dtype=jnp.int32)[None, :])
    ranked = jnp.cumsum(member.astype(jnp.int32), axis=0) - 1
    return jnp.sum(jnp.where(member, ranked, 0), axis=1)


def stepwise(density, anchor, feeds, turns, plan, capacity_levels):
    num_cells, num_links, commodity_width = density.shape
    peers = lax.axis_size("region")
    my_region = lax.axis_index("region")
    bucket = 4 * max(1, (num_links // 2 + 4 * (peers - 2) - 1) // (4 * (peers - 2)))
    flat_feed = feeds.reshape(-1)
    flat_turn = turns.reshape(-1)
    is_live = flat_feed >= 0
    owners = jnp.where(is_live, flat_feed // num_links, -1)
    local_ids = jnp.where(is_live, flat_feed % num_links, 0)
    is_remote = is_live & (owners != my_region)
    is_nearby = is_live & (owners == my_region)
    capacity = 2 * bucket
    slots = slot_ranks(is_remote, owners, peers)
    total_slots = peers * capacity
    leader_flat = jnp.where(is_remote, owners * capacity + slots, -1)
    route_flat = jnp.where(is_remote, owners * capacity + slots, -1)
    leader_table = one_hot_table(leader_flat, total_slots)
    route_table = one_hot_table(route_flat, total_slots)
    id_filled = table_total(local_ids, leader_table)
    request_ids = jnp.where(jnp.any(leader_table, axis=0), id_filled, -1).reshape(peers, capacity)
    request_counts = table_total(flat_turn, route_table).reshape(peers, capacity)
    asked_ids, asked_counts = (
        lax.all_to_all(request_ids, "region", split_axis=0, concat_axis=0, tiled=True),
        lax.all_to_all(request_counts, "region", split_axis=0, concat_axis=0, tiled=True),
    )
    flat_asked = asked_ids.reshape(-1)
    nearby_rows = jnp.where(is_nearby, local_ids, -1)
    nearby_table = one_hot_table(nearby_rows, num_links)
    asked_table = one_hot_table(flat_asked, num_links)
    count_total = table_total(jnp.where(is_nearby, flat_turn, 0), nearby_table)
    count_total = count_total + table_total(asked_counts.reshape(-1), asked_table)
    denominator = count_total.astype(jnp.float32) + EXIT_WEIGHT
    gather_ids = jnp.maximum(flat_asked, 0)
    pick_peer = jnp.where(is_remote, owners, 0)
    pick_slot = jnp.where(is_remote, slots, 0)
    live_weight = jnp.where(is_live, flat_turn, 0).astype(jnp.float32)
    level_ids = jnp.arange(capacity_levels.shape[0], dtype=jnp.int32)
    cell_sum, anchor_total = lax.psum((jnp.sum(density, axis=2), jnp.sum(anchor, axis=1)), "dest")
    for step_index in range(plan.shape[0]):
        last_rows = density[num_cells - 1]
        if step_index > 0:
            cell_sum = lax.psum(jnp.sum(density, axis=2), "dest")
        level_match = plan[step_index][:, None] == level_ids[None, :]
        capacity_now = jnp.sum(jnp.where(level_match, capacity_levels[None, :], 0.0), axis=1) * COMM
        sending = jnp.minimum(FREE_SPEED * cell_sum, capacity_now[None, :])
        receiving = jnp.minimum(capacity_now[None, :], WAVE_SPEED * (JAM_FACTOR * COMM - cell_sum))
        per_count = sending[num_cells - 1] / denominator
        unit_share = per_count / cell_sum[num_cells - 1]
        sent_count = per_count[gather_ids].reshape(peers, capacity)
        sent_unit = unit_share[gather_ids].reshape(peers, capacity)
        sent_rows = last_rows[gather_ids].reshape(peers, capacity, commodity_width)
        got_rows, got_count, got_unit = (
            lax.all_to_all(sent_rows, "region", split_axis=0, concat_axis=0, tiled=True),
            lax.all_to_all(sent_count, "region", split_axis=0, concat_axis=0, tiled=True),
            lax.all_to_all(sent_unit, "region", split_axis=0, concat_axis=0, tiled=True),
        )
        pair_count = jnp.where(is_remote, got_count[pick_peer, pick_slot], per_count[local_ids])
        pair_unit = jnp.where(is_remote, got_unit[pick_peer, pick_slot], unit_share[local_ids])
        pair_rows = jnp.where(
            is_remote[:, None], got_rows[pick_peer, pick_slot], last_rows[local_ids]
        )
        demand = jnp.sum((live_weight * pair_count).reshape(num_links, 4), axis=1) + anchor_total
        ratio = receiving[0] / jnp.maximum(receiving[0], demand)
        mixing = (live_weight * pair_unit).reshape(num_links, 4)
        gathered = jnp.sum(
            mixing[:, :, None] * pair_rows.reshape(num_links, 4, commodity_width), axis=1
        )
        inflow = ratio[:, None] * (gathered + anchor)
        granted = (live_weight.reshape(num_links, 4) * ratio[:, None]).reshape(-1)
        send_back = table_total(granted, route_table).reshape(peers, capacity)
        returned = lax.all_to_all(send_back, "region", split_axis=0, concat_axis=0, tiled=True)
        passed = table_total(jnp.where(is_nearby, granted, 0.0), nearby_table)
        passed = passed + table_total(returned.reshape(-1), asked_table)
        outflow = (unit_share * (passed + EXIT_WEIGHT))[:, None] * last_rows
        through = jnp.minimum(sending[:-1], receiving[1:])
        moving = (through / cell_sum[:-1])[:, :, None] * density[:-1]
        density = (
            density
            - jnp.pad(moving, ((0, 1), (0, 0), (0, 0)))
            + jnp.pad(moving, ((1, 0), (0, 0), (0, 0)))
        )
        density = jnp.concatenate(
            [
                density[:1] + inflow[None],
                density[1 : num_cells - 1],
                density[num_cells - 1 :] - outflow[None],
            ],
            axis=0,
        )
    return density


def split_two(values):
    high = values.astype(jnp.bfloat16)
    low = (values - high.astype(jnp.float32)).astype(jnp.bfloat16)
    return high, low


def dot(a, b, dims):
    return lax.dot_general(a, b, (dims, ((), ())), preferred_element_type=jnp.float32)


NN = ((1,), (0,))
NT = ((1,), (1,))


def vector_dot(row, matrix, dims):
    first = row.astype(jnp.bfloat16).astype(jnp.float32)
    second = (row - first).astype(jnp.bfloat16).astype(jnp.float32)
    third = row - first - second
    at = lax.broadcasted_iota(jnp.int32, (16, row.shape[1]), 0)
    stacked = jnp.where(at == 0, first, jnp.where(at == 1, second, jnp.where(at == 2, third, 0.0)))
    return jnp.sum(dot(stacked.astype(jnp.bfloat16), matrix, dims), axis=0, keepdims=True)


def network_kernel(
    regions, shares, slots, steps,
    density_ref, anchor_ref, ints_ref, levels_ref, out_ref,
    ints_all, parts, totals, matrix, keys, rows_out, rows_in, weights, coefs, columns,
    int_send, int_recv, part_send, part_recv, total_send, total_recv, row_send, row_recv,
):
    cells, links, width = density_ref.shape
    all_links = regions * links
    held = regions * slots
    me = lax.axis_index("region")
    share = lax.axis_index("dest")
    mine = pl.ds(pl.multiple_of(me * links, links), links)

    def region_at(offset):
        return lax.rem(me + offset, regions)

    def lanes(region):
        return pl.ds(pl.multiple_of(region * links, links), links)

    def slot_rows(region):
        return pl.ds(pl.multiple_of(region * slots, slots), slots)

    def to_region(src, dst, send, recv, offset):
        return pltpu.make_async_remote_copy(
            src_ref=src, dst_ref=dst, send_sem=send.at[offset], recv_sem=recv.at[offset],
            device_id={"region": region_at(offset)}, device_id_type=pl.DeviceIdType.MESH,
        )

    barrier = pltpu.get_barrier_semaphore()
    for offset in range(1, regions):
        pl.semaphore_signal(barrier, inc=1, device_id={"region": region_at(offset)}, device_id_type=pl.DeviceIdType.MESH)
    for offset in range(1, shares):
        pl.semaphore_signal(
            barrier, inc=1, device_id={"dest": lax.rem(share + offset, shares)}, device_id_type=pl.DeviceIdType.MESH
        )

    ints_all[:, mine] = ints_ref[...]
    summed = jnp.zeros((16, links), jnp.float32)
    pick = lax.broadcasted_iota(jnp.int32, (16, width), 0)
    for cell in range(cells + 1):
        high, low = split_two(density_ref[cell] if cell < cells else anchor_ref[...])
        ones = jnp.where(pick == cell, 1.0, 0.0).astype(jnp.bfloat16)
        summed = summed + dot(ones, high, NT) + dot(ones, low, NT)
    parts[share] = summed
    rows_in[:, slot_rows(me), :] = jnp.zeros((steps, slots, width), jnp.float32)
    coefs[...] = jnp.zeros_like(coefs)

    pl.semaphore_wait(barrier, regions + shares - 2)
    int_copies, part_copies, total_copies, row_copies = [], [], [], []
    for offset in range(1, regions):
        copy = to_region(ints_all.at[:, mine], ints_all.at[:, mine], int_send, int_recv, offset)
        copy.start()
        int_copies.append(copy)
    for offset in range(1, shares):
        copy = pltpu.make_async_remote_copy(
            src_ref=parts.at[share], dst_ref=parts.at[share],
            send_sem=part_send.at[offset], recv_sem=part_recv.at[offset],
            device_id={"dest": lax.rem(share + offset, shares)}, device_id_type=pl.DeviceIdType.MESH,
        )
        copy.start()
        part_copies.append(copy)

    for copy in int_copies:
        copy.wait()
    for block in range(regions):
        named = lax.broadcasted_iota(jnp.int32, (links, all_links), 0) + block * links
        count = jnp.zeros((links, all_links), jnp.float32)
        for entry in range(4):
            count = count + jnp.where(
                ints_all[entry : entry + 1, :] == named, ints_all[4 + entry : 5 + entry, :].astype(jnp.float32), 0.0
            )
        matrix[block * links : (block + 1) * links, :] = count.astype(jnp.bfloat16)

    region_row = lax.broadcasted_iota(jnp.int32, (16, all_links), 0)
    link_column = lax.broadcasted_iota(jnp.int32, (16, all_links), 1)
    member = jnp.where(link_column // links == region_row, 1.0, 0.0).astype(jnp.bfloat16)
    taken = dot(member, matrix[...], NT)
    denominator = jnp.sum(taken, axis=0, keepdims=True) + EXIT_WEIGHT
    before = lax.broadcasted_iota(jnp.int32, (links, links), 0) < lax.broadcasted_iota(jnp.int32, (links, links), 1)
    before = jnp.where(before, 1.0, 0.0).astype(jnp.bfloat16)
    named_at = jnp.where(taken > 0.0, 1.0, 0.0)
    for block in range(regions):
        at = slice(block * links, (block + 1) * links)
        rank = dot(named_at[:, at].astype(jnp.bfloat16), before, NN)
        keys[:, at] = jnp.where(named_at[:, at] > 0.0, rank, -1.0)

    for copy in part_copies:
        copy.wait()
    total_here = parts[0]
    for other in range(1, shares):
        total_here = total_here + parts[other]
    totals[:, mine] = total_here
    for offset in range(1, regions):
        copy = to_region(totals.at[:, mine], totals.at[:, mine], total_send, total_recv, offset)
        copy.start()
        total_copies.append(copy)

    own_keys = keys[:, mine]
    slot_at = lax.broadcasted_iota(jnp.int32, (slots, links), 0).astype(jnp.float32)
    chosen = jnp.concatenate(
        [jnp.where(own_keys[region : region + 1] == slot_at, 1.0, 0.0) for region in range(regions)], axis=0
    ).astype(jnp.bfloat16)
    for back in range(steps):
        high, low = split_two(density_ref[cells - 1 - back])
        rows_out[back] = dot(chosen, high, NN) + dot(chosen, low, NN)
    for offset in range(1, regions):
        copy = to_region(
            rows_out.at[:, slot_rows(region_at(offset)), :], rows_in.at[:, slot_rows(me), :], row_send, row_recv, offset
        )
        copy.start()
        row_copies.append(copy)

    wanted = jnp.sum(jnp.where(region_row == me, keys[...], 0.0), axis=0, keepdims=True)
    lane = lax.broadcasted_iota(jnp.int32, (1, all_links), 1)
    wanted = jnp.where(
        (wanted >= 0.0) & (lane // links != me), wanted + (lane // links * slots).astype(jnp.float32), -1.0
    )
    held_at = jnp.where(
        lax.broadcasted_iota(jnp.int32, (held, all_links), 0).astype(jnp.float32) == wanted, 1.0, 0.0
    ).astype(jnp.bfloat16)
    far_counts = jnp.transpose(dot(held_at, matrix[:, mine], NN))
    near_counts = jnp.transpose(matrix[mine, mine].astype(jnp.float32))

    for copy in total_copies:
        copy.wait()
    cell_row = lax.broadcasted_iota(jnp.int32, (cells, all_links), 0)

    def moved_up(values):
        return jnp.where(cell_row == 0, 0.0, pltpu.roll(values, 1, 0))

    total = totals[0:cells, :]
    anchor_total = totals[cells : cells + 1, :]
    kept = [jnp.ones((cells, all_links), jnp.float32)]
    entered = []
    weight_rows = []
    for step in range(steps):
        plan_row = ints_all[8 + step : 9 + step, :]
        capacity = jnp.zeros((1, all_links), jnp.float32)
        for level in range(levels_ref.shape[0]):
            capacity = jnp.where(plan_row == level, levels_ref[level], capacity)
        capacity = capacity * COMM
        sending = jnp.minimum(FREE_SPEED * total, capacity)
        receiving = jnp.minimum(capacity, WAVE_SPEED * (JAM_FACTOR * COMM - total))
        per_count = sending[cells - 1 : cells] / denominator
        unit_share = per_count / total[cells - 1 : cells]
        demand = vector_dot(per_count, matrix[...], NN) + anchor_total
        ratio = receiving[0:1] / jnp.maximum(receiving[0:1], demand)
        passed = vector_dot(ratio, matrix[...], NT)
        leaving = unit_share * (passed + EXIT_WEIGHT)
        through = jnp.where(cell_row < cells - 1, jnp.minimum(sending, pltpu.roll(receiving, cells - 1, 0)), 0.0)
        going = through / total
        staying = 1.0 - going - jnp.where(cell_row == cells - 1, leaving, 0.0)
        weight_rows += [unit_share * part[cells - 1 : cells] for part in kept]
        total = (
            total - through + moved_up(through)
            + jnp.where(cell_row == 0, ratio * demand, 0.0)
            - jnp.where(cell_row == cells - 1, leaving * total, 0.0)
        )
        zero = jnp.zeros((cells, all_links), jnp.float32)
        kept = [
            staying * same + moved_up(going * above) for same, above in zip(kept + [zero], [zero] + kept)
        ]
        entered = [staying * part + moved_up(going * part) for part in entered]
        entered.append(jnp.where(cell_row == 0, ratio, 0.0))

    for index, row in enumerate(weight_rows):
        weights[index : index + 1, :] = row
    blocks = kept + entered + [functools.reduce(lambda a, b: a + b, entered)]
    for index, block in enumerate(blocks):
        coefs[index * cells : (index + 1) * cells, :] = block
    columns[...] = jnp.transpose(coefs[:, mine])

    def column(block, cell):
        at = block * cells + cell
        return columns[:, at : at + 1]

    weight_high, weight_low = split_two(weights[...])
    far_weights = dot(weight_high, held_at, NT) + dot(weight_low, held_at, NT)
    near_weights = weights[:, mine]

    def mixed(counts, row_weights, content):
        results = []
        for step in range(steps):
            gathered = None
            for back in range(step + 1):
                index = step * (step + 1) // 2 + back
                high, low = split_two(counts * row_weights[index : index + 1])
                content_high, content_low = content[back]
                term = dot(high, content_high, NN) + dot(low, content_high, NN) + dot(high, content_low, NN)
                gathered = term if gathered is None else gathered + term
            results.append(gathered)
        return results

    near = mixed(near_counts, near_weights, [split_two(density_ref[cells - 1 - back]) for back in range(steps)])
    for cell in range(cells - 1, -1, -1):
        value = column(0, cell) * density_ref[cell]
        for back in range(1, min(steps, cell) + 1):
            value = value + column(back, cell) * density_ref[cell - back]
        if cell < steps:
            value = value + column(2 * steps + 1, cell) * anchor_ref[...]
            for step in range(steps - cell):
                value = value + column(steps + 1 + step, cell) * near[step]
        out_ref[cell] = value

    for copy in row_copies:
        copy.wait()
    far = mixed(far_counts, far_weights, [split_two(rows_in[back]) for back in range(steps)])
    for cell in range(steps):
        value = out_ref[cell]
        for step in range(steps - cell):
            value = value + column(steps + 1 + step, cell) * far[step]
        out_ref[cell] = value


def fused(density, anchor, feeds, turns, plan, capacity_levels):
    cells, links, width = density.shape
    steps = plan.shape[0]
    regions = lax.axis_size("region")
    shares = lax.axis_size("dest")
    slots = slot_bound(links, regions)
    all_links = regions * links
    ints = jnp.concatenate(
        [feeds.T, turns.T, plan, jnp.zeros((8 - steps, links), jnp.int32)], axis=0
    )
    vmem = pl.BlockSpec(memory_space=pltpu.VMEM)
    return pl.pallas_call(
        functools.partial(network_kernel, regions, shares, slots, steps),
        out_shape=jax.ShapeDtypeStruct(density.shape, jnp.float32),
        in_specs=[vmem, vmem, vmem, pl.BlockSpec(memory_space=pltpu.SMEM)],
        out_specs=vmem,
        scratch_shapes=[
            pltpu.VMEM((16, all_links), jnp.int32),
            pltpu.VMEM((shares, 16, links), jnp.float32),
            pltpu.VMEM((16, all_links), jnp.float32),
            pltpu.VMEM((all_links, all_links), jnp.bfloat16),
            pltpu.VMEM((16, all_links), jnp.float32),
            pltpu.VMEM((steps, regions * slots, width), jnp.float32),
            pltpu.VMEM((steps, regions * slots, width), jnp.float32),
            pltpu.VMEM((8, all_links), jnp.float32),
            pltpu.VMEM((128, all_links), jnp.float32),
            pltpu.VMEM((links, 128), jnp.float32),
        ]
        + [pltpu.SemaphoreType.DMA((regions,))] * 2
        + [pltpu.SemaphoreType.DMA((shares,))] * 2
        + [pltpu.SemaphoreType.DMA((regions,))] * 4,
        compiler_params=pltpu.CompilerParams(
            collective_id=0, has_side_effects=True, vmem_limit_bytes=32 * 1024 * 1024
        ),
    )(density, anchor, ints, capacity_levels)


def slot_bound(links, regions):
    return 4 * max(1, (links // 2 + 4 * (regions - 2) - 1) // (4 * (regions - 2)))


def local(density, *rest):
    regions = lax.axis_size("region")
    links = density.shape[1]
    if regions * links <= 1024 and regions * slot_bound(links, regions) == 128:
        return fused(density, *rest)
    return stepwise(density, *rest)


def solution(mesh):
    in_specs = (
        P(None, ("scen", "region"), "dest"),
        P(("scen", "region"), "dest"),
        P("region", None),
        P("region", None),
        P(None, "region"),
        P(),
    )
    out_specs = P(None, ("scen", "region"), "dest")
    return jax.shard_map(local, mesh=mesh, in_specs=in_specs, out_specs=out_specs, check_vma=False)
```

```python
import functools

import jax
import jax.numpy as jnp
from jax import lax
from jax.experimental import pallas as pl
from jax.experimental.pallas import tpu as pltpu
from jax.sharding import PartitionSpec as P

COMM = 1024


FREE_SPEED = 0.8
WAVE_SPEED = 0.4
JAM_FACTOR = 2.0
EXIT_WEIGHT = 4.0


def one_hot_table(positions, segments):
    return positions[:, None] == jnp.arange(segments, dtype=jnp.int32)[None, :]


def table_total(values, table):
    return jnp.sum(jnp.where(table, values[:, None], 0), axis=0)


def slot_ranks(chosen, owners, peers):
    member = chosen[:, None] & (owners[:, None] == jnp.arange(peers, dtype=jnp.int32)[None, :])
    ranked = jnp.cumsum(member.astype(jnp.int32), axis=0) - 1
    return jnp.sum(jnp.where(member, ranked, 0), axis=1)


def stepwise(density, anchor, feeds, turns, plan, capacity_levels):
    num_cells, num_links, commodity_width = density.shape
    peers = lax.axis_size("region")
    my_region = lax.axis_index("region")
    bucket = 4 * max(1, (num_links // 2 + 4 * (peers - 2) - 1) // (4 * (peers - 2)))
    flat_feed = feeds.reshape(-1)
    flat_turn = turns.reshape(-1)
    is_live = flat_feed >= 0
    owners = jnp.where(is_live, flat_feed // num_links, -1)
    local_ids = jnp.where(is_live, flat_feed % num_links, 0)
    is_remote = is_live & (owners != my_region)
    is_nearby = is_live & (owners == my_region)
    capacity = 2 * bucket
    slots = slot_ranks(is_remote, owners, peers)
    total_slots = peers * capacity
    leader_flat = jnp.where(is_remote, owners * capacity + slots, -1)
    route_flat = jnp.where(is_remote, owners * capacity + slots, -1)
    leader_table = one_hot_table(leader_flat, total_slots)
    route_table = one_hot_table(route_flat, total_slots)
    id_filled = table_total(local_ids, leader_table)
    request_ids = jnp.where(jnp.any(leader_table, axis=0), id_filled, -1).reshape(peers, capacity)
    request_counts = table_total(flat_turn, route_table).reshape(peers, capacity)
    asked_ids, asked_counts = (
        lax.all_to_all(request_ids, "region", split_axis=0, concat_axis=0, tiled=True),
        lax.all_to_all(request_counts, "region", split_axis=0, concat_axis=0, tiled=True),
    )
    flat_asked = asked_ids.reshape(-1)
    nearby_rows = jnp.where(is_nearby, local_ids, -1)
    nearby_table = one_hot_table(nearby_rows, num_links)
    asked_table = one_hot_table(flat_asked, num_links)
    count_total = table_total(jnp.where(is_nearby, flat_turn, 0), nearby_table)
    count_total = count_total + table_total(asked_counts.reshape(-1), asked_table)
    denominator = count_total.astype(jnp.float32) + EXIT_WEIGHT
    gather_ids = jnp.maximum(flat_asked, 0)
    pick_peer = jnp.where(is_remote, owners, 0)
    pick_slot = jnp.where(is_remote, slots, 0)
    live_weight = jnp.where(is_live, flat_turn, 0).astype(jnp.float32)
    level_ids = jnp.arange(capacity_levels.shape[0], dtype=jnp.int32)
    cell_sum, anchor_total = lax.psum((jnp.sum(density, axis=2), jnp.sum(anchor, axis=1)), "dest")
    for step_index in range(plan.shape[0]):
        last_rows = density[num_cells - 1]
        if step_index > 0:
            cell_sum = lax.psum(jnp.sum(density, axis=2), "dest")
        level_match = plan[step_index][:, None] == level_ids[None, :]
        capacity_now = jnp.sum(jnp.where(level_match, capacity_levels[None, :], 0.0), axis=1) * COMM
        sending = jnp.minimum(FREE_SPEED * cell_sum, capacity_now[None, :])
        receiving = jnp.minimum(capacity_now[None, :], WAVE_SPEED * (JAM_FACTOR * COMM - cell_sum))
        per_count = sending[num_cells - 1] / denominator
        unit_share = per_count / cell_sum[num_cells - 1]
        sent_count = per_count[gather_ids].reshape(peers, capacity)
        sent_unit = unit_share[gather_ids].reshape(peers, capacity)
        sent_rows = last_rows[gather_ids].reshape(peers, capacity, commodity_width)
        got_rows, got_count, got_unit = (
            lax.all_to_all(sent_rows, "region", split_axis=0, concat_axis=0, tiled=True),
            lax.all_to_all(sent_count, "region", split_axis=0, concat_axis=0, tiled=True),
            lax.all_to_all(sent_unit, "region", split_axis=0, concat_axis=0, tiled=True),
        )
        pair_count = jnp.where(is_remote, got_count[pick_peer, pick_slot], per_count[local_ids])
        pair_unit = jnp.where(is_remote, got_unit[pick_peer, pick_slot], unit_share[local_ids])
        pair_rows = jnp.where(
            is_remote[:, None], got_rows[pick_peer, pick_slot], last_rows[local_ids]
        )
        demand = jnp.sum((live_weight * pair_count).reshape(num_links, 4), axis=1) + anchor_total
        ratio = receiving[0] / jnp.maximum(receiving[0], demand)
        mixing = (live_weight * pair_unit).reshape(num_links, 4)
        gathered = jnp.sum(
            mixing[:, :, None] * pair_rows.reshape(num_links, 4, commodity_width), axis=1
        )
        inflow = ratio[:, None] * (gathered + anchor)
        granted = (live_weight.reshape(num_links, 4) * ratio[:, None]).reshape(-1)
        send_back = table_total(granted, route_table).reshape(peers, capacity)
        returned = lax.all_to_all(send_back, "region", split_axis=0, concat_axis=0, tiled=True)
        passed = table_total(jnp.where(is_nearby, granted, 0.0), nearby_table)
        passed = passed + table_total(returned.reshape(-1), asked_table)
        outflow = (unit_share * (passed + EXIT_WEIGHT))[:, None] * last_rows
        through = jnp.minimum(sending[:-1], receiving[1:])
        moving = (through / cell_sum[:-1])[:, :, None] * density[:-1]
        density = (
            density
            - jnp.pad(moving, ((0, 1), (0, 0), (0, 0)))
            + jnp.pad(moving, ((1, 0), (0, 0), (0, 0)))
        )
        density = jnp.concatenate(
            [
                density[:1] + inflow[None],
                density[1 : num_cells - 1],
                density[num_cells - 1 :] - outflow[None],
            ],
            axis=0,
        )
    return density


def split_two(values):
    high = values.astype(jnp.bfloat16)
    low = (values - high.astype(jnp.float32)).astype(jnp.bfloat16)
    return high, low


def dot(a, b, dims):
    return lax.dot_general(a, b, (dims, ((), ())), preferred_element_type=jnp.float32)


NN = ((1,), (0,))
NT = ((1,), (1,))


def vector_dot(row, matrix, dims):
    first = row.astype(jnp.bfloat16).astype(jnp.float32)
    second = (row - first).astype(jnp.bfloat16).astype(jnp.float32)
    third = row - first - second
    at = lax.broadcasted_iota(jnp.int32, (16, row.shape[1]), 0)
    stacked = jnp.where(at == 0, first, jnp.where(at == 1, second, jnp.where(at == 2, third, 0.0)))
    return jnp.sum(dot(stacked.astype(jnp.bfloat16), matrix, dims), axis=0, keepdims=True)


def across(index, mask):
    bit = 1
    while bit <= mask:
        if mask & bit:
            index = index + bit - 2 * bit * lax.rem(index // bit, 2)
        bit *= 2
    return index


def network_kernel(
    regions, shares, slots, steps,
    density_hbm, anchor_hbm, feeds_hbm, turns_hbm, plan_hbm, levels_hbm, out_hbm,
    density_ref, anchor_ref, feeds_ref, turns_ref, plan_ref, levels_ref, out_ref,
    ints_all, asking, asked, parts, totals, matrix, keys, rows_out, rows_in, weights, coefs, columns,
    in_sem, out_sem, int_send, int_recv, key_send, key_recv, part_send, part_recv, total_send, total_recv, row_send, row_recv,
):
    cells, links, width = density_ref.shape
    all_links = regions * links
    held = regions * slots
    me = lax.axis_index("region")
    share = lax.axis_index("dest")

    def lanes(region):
        return pl.ds(pl.multiple_of(region * links, links), links)

    def slot_rows(region):
        return pl.ds(pl.multiple_of(region * slots, slots), slots)

    mine = lanes(me)

    def start_all(copies):
        for copy in copies:
            copy.start()
        return copies

    def wait_all(copies):
        for copy in copies:
            copy.wait()

    def to_region(src, dst, send, recv, mask):
        return pltpu.make_async_remote_copy(
            src_ref=src, dst_ref=dst, send_sem=send.at[mask], recv_sem=recv.at[mask],
            device_id={"region": across(me, mask)}, device_id_type=pl.DeviceIdType.MESH,
        )

    masks = list(range(regions // 2, regions)) + list(range(regions // 2 - 1, 0, -1))

    barrier = pltpu.get_barrier_semaphore()
    for mask in masks:
        pl.semaphore_signal(barrier, inc=1, device_id={"region": across(me, mask)}, device_id_type=pl.DeviceIdType.MESH)
    for mask in range(1, shares):
        pl.semaphore_signal(barrier, inc=1, device_id={"dest": across(share, mask)}, device_id_type=pl.DeviceIdType.MESH)

    small = start_all([
        pltpu.make_async_copy(src, dst, in_sem.at[at]) for at, (src, dst) in enumerate(
            [(feeds_hbm, feeds_ref), (turns_hbm, turns_ref), (plan_hbm, plan_ref), (levels_hbm, levels_ref)])
    ])
    anchor_copy = pltpu.make_async_copy(anchor_hbm, anchor_ref, in_sem.at[4])
    cell_copies = {
        cell: pltpu.make_async_copy(density_hbm.at[cell], density_ref.at[cell], in_sem.at[5 + cell])
        for cell in range(cells - 1, -1, -1)
    }
    start_all(list(cell_copies.values()) + [anchor_copy])
    rows_in[:, slot_rows(me), :] = jnp.zeros((steps, slots, width), jnp.float32)
    asked[me] = jnp.full((8, links), -1.0, jnp.float32)
    coefs[...] = jnp.zeros_like(coefs)
    wait_all(small)

    def counts_of(feeds, turns):
        named = lax.broadcasted_iota(jnp.int32, (all_links, links), 0)
        count = jnp.zeros((all_links, links), jnp.float32)
        for entry in range(4):
            count = count + jnp.where(
                feeds[entry : entry + 1] == named, turns[entry : entry + 1].astype(jnp.float32), 0.0
            )
        return count.astype(jnp.bfloat16)

    ints_all[0:4, mine] = feeds_ref[...]
    ints_all[4:8, mine] = turns_ref[...]
    ints_all[8 : 8 + steps, mine] = plan_ref[...]
    own_counts = counts_of(feeds_ref[...], turns_ref[...])
    matrix[:, mine] = own_counts
    named_at = jnp.where(dot(jnp.ones((16, links), jnp.bfloat16), own_counts, NT) > 0.0, 1.0, 0.0)
    before = lax.broadcasted_iota(jnp.int32, (links, links), 0) < lax.broadcasted_iota(jnp.int32, (links, links), 1)
    before = jnp.where(before, 1.0, 0.0).astype(jnp.bfloat16)
    for block in range(regions):
        at = slice(block * links, (block + 1) * links)
        rank = dot(named_at[:, at].astype(jnp.bfloat16), before, NN)
        key = jnp.where(named_at[:, at] > 0.0, rank, -1.0)
        keys[:, at] = key
        asking[block] = key[0:8]

    summed = jnp.zeros((16, links), jnp.float32)
    pick = lax.broadcasted_iota(jnp.int32, (16, width), 0)
    for cell in list(cell_copies) + [cells]:
        if cell < cells:
            cell_copies[cell].wait()
        else:
            anchor_copy.wait()
        high, low = split_two(density_ref[cell] if cell < cells else anchor_ref[...])
        ones = jnp.where(pick == cell, 1.0, 0.0).astype(jnp.bfloat16)
        summed = summed + dot(ones, high, NT) + dot(ones, low, NT)
    parts[share] = summed

    pl.semaphore_wait(barrier, regions + shares - 2)
    key_copies = start_all([
        to_region(asking.at[across(me, mask)], asked.at[me], key_send, key_recv, mask) for mask in masks
    ])
    part_copies = start_all([
        pltpu.make_async_remote_copy(
            src_ref=parts.at[share], dst_ref=parts.at[share],
            send_sem=part_send.at[mask], recv_sem=part_recv.at[mask],
            device_id={"dest": across(share, mask)}, device_id_type=pl.DeviceIdType.MESH,
        )
        for mask in range(1, shares)
    ])
    int_copies = start_all([
        to_region(ints_all.at[:, mine], ints_all.at[:, mine], int_send, int_recv, mask) for mask in masks
    ])

    lane = lax.broadcasted_iota(jnp.int32, (1, all_links), 1)
    wanted = keys[0:1, :]
    wanted = jnp.where(
        (wanted >= 0.0) & (lane // links != me), wanted + (lane // links * slots).astype(jnp.float32), -1.0
    )
    held_at = jnp.where(
        lax.broadcasted_iota(jnp.int32, (held, all_links), 0).astype(jnp.float32) == wanted, 1.0, 0.0
    ).astype(jnp.bfloat16)
    far_counts = jnp.transpose(dot(held_at, own_counts, NN))
    near_counts = jnp.transpose(matrix[mine, mine].astype(jnp.float32))

    wait_all(part_copies)
    total_here = parts[0]
    for other in range(1, shares):
        total_here = total_here + parts[other]
    totals[:, mine] = total_here
    total_copies = start_all([
        to_region(totals.at[:, mine], totals.at[:, mine], total_send, total_recv, mask) for mask in masks
    ])

    wait_all(key_copies)
    slot_at = lax.broadcasted_iota(jnp.int32, (slots, links), 0).astype(jnp.float32)
    chosen = jnp.concatenate(
        [jnp.where(asked[region, 0:1, :] == slot_at, 1.0, 0.0) for region in range(regions)], axis=0
    ).astype(jnp.bfloat16)
    row_copies = []
    for back in range(steps):
        high, low = split_two(density_ref[cells - 1 - back])
        rows_out[back] = dot(chosen, high, NN) + dot(chosen, low, NN)
        row_copies.append(start_all([
            to_region(
                rows_out.at[back, slot_rows(across(me, mask)), :], rows_in.at[back, slot_rows(me), :],
                row_send.at[back], row_recv.at[back], mask,
            )
            for mask in masks
        ]))

    wait_all(int_copies)
    for mask in masks:
        theirs = lanes(across(me, mask))
        matrix[:, theirs] = counts_of(ints_all[0:4, theirs], ints_all[4:8, theirs])
    denominator = dot(jnp.ones((16, all_links), jnp.bfloat16), matrix[...], NT)[0:1] + EXIT_WEIGHT

    wait_all(total_copies)
    cell_row = lax.broadcasted_iota(jnp.int32, (cells, all_links), 0)

    def moved_up(values):
        return jnp.where(cell_row == 0, 0.0, pltpu.roll(values, 1, 0))

    total = totals[0:cells, :]
    anchor_total = totals[cells : cells + 1, :]
    kept = [jnp.ones((cells, all_links), jnp.float32)]
    entered = []
    weight_rows = []
    for step in range(steps):
        plan_row = ints_all[8 + step : 9 + step, :]
        capacity = jnp.zeros((1, all_links), jnp.float32)
        for level in range(levels_ref.shape[0]):
            capacity = jnp.where(plan_row == level, levels_ref[level], capacity)
        capacity = capacity * COMM
        sending = jnp.minimum(FREE_SPEED * total, capacity)
        receiving = jnp.minimum(capacity, WAVE_SPEED * (JAM_FACTOR * COMM - total))
        per_count = sending[cells - 1 : cells] / denominator
        unit_share = per_count / total[cells - 1 : cells]
        demand = vector_dot(per_count, matrix[...], NN) + anchor_total
        ratio = receiving[0:1] / jnp.maximum(receiving[0:1], demand)
        passed = vector_dot(ratio, matrix[...], NT)
        leaving = unit_share * (passed + EXIT_WEIGHT)
        through = jnp.where(cell_row < cells - 1, jnp.minimum(sending, pltpu.roll(receiving, cells - 1, 0)), 0.0)
        going = through / total
        staying = 1.0 - going - jnp.where(cell_row == cells - 1, leaving, 0.0)
        weight_rows += [unit_share * part[cells - 1 : cells] for part in kept]
        total = (
            total - through + moved_up(through)
            + jnp.where(cell_row == 0, ratio * demand, 0.0)
            - jnp.where(cell_row == cells - 1, leaving * total, 0.0)
        )
        zero = jnp.zeros((cells, all_links), jnp.float32)
        kept = [
            staying * same + moved_up(going * above) for same, above in zip(kept + [zero], [zero] + kept)
        ]
        entered = [staying * part + moved_up(going * part) for part in entered]
        entered.append(jnp.where(cell_row == 0, ratio, 0.0))

    for index, row in enumerate(weight_rows):
        weights[index : index + 1, :] = row
    blocks = kept + entered + [functools.reduce(lambda a, b: a + b, entered)]
    for index, block in enumerate(blocks):
        coefs[index * cells : (index + 1) * cells, :] = block
    columns[...] = jnp.transpose(coefs[:, mine])

    def column(block, cell):
        at = block * cells + cell
        return columns[:, at : at + 1]

    weight_high, weight_low = split_two(weights[...])
    far_weights = dot(weight_high, held_at, NT) + dot(weight_low, held_at, NT)
    near_weights = weights[:, mine]

    def mixing(counts, row_weights, back):
        pieces = []
        for cell in range(steps - back):
            piece = None
            for step in range(back, steps - cell):
                index = step * (step + 1) // 2 + back
                term = column(steps + 1 + step, cell) * row_weights[index : index + 1]
                piece = term if piece is None else piece + term
            pieces.append(counts * piece)
        return split_two(jnp.concatenate(pieces, axis=0))

    def mixed(mixing_pair, content):
        high, low = mixing_pair
        content_high, content_low = split_two(content)
        return dot(high, content_high, NN) + dot(low, content_high, NN) + dot(high, content_low, NN)

    far_mixing = [mixing(far_counts, far_weights, back) for back in range(steps)]
    near = [
        mixed(mixing(near_counts, near_weights, back), density_ref[cells - 1 - back]) for back in range(steps)
    ]
    out_copies = [
        pltpu.make_async_copy(out_ref.at[cell], out_hbm.at[cell], out_sem.at[cell]) for cell in range(cells)
    ]
    for cell in range(cells):
        value = column(0, cell) * density_ref[cell]
        for back in range(1, min(steps, cell) + 1):
            value = value + column(back, cell) * density_ref[cell - back]
        if cell < steps:
            value = value + column(2 * steps + 1, cell) * anchor_ref[...]
            for back in range(steps - cell):
                value = value + near[back][cell * links : (cell + 1) * links]
        out_ref[cell] = value
        if cell >= steps:
            out_copies[cell].start()

    for back in range(steps):
        wait_all(row_copies[back])
        far = mixed(far_mixing[back], rows_in[back])
        for cell in range(steps - back):
            out_ref[cell] = out_ref[cell] + far[cell * links : (cell + 1) * links]
        out_copies[steps - back - 1].start()
    wait_all(out_copies)


def fused(density, anchor, feeds, turns, plan, capacity_levels):
    cells, links, width = density.shape
    steps = plan.shape[0]
    regions = lax.axis_size("region")
    shares = lax.axis_size("dest")
    slots = slot_bound(links, regions)
    all_links = regions * links
    hbm = pl.BlockSpec(memory_space=pltpu.HBM)
    return pl.pallas_call(
        functools.partial(network_kernel, regions, shares, slots, steps),
        out_shape=jax.ShapeDtypeStruct(density.shape, jnp.float32),
        in_specs=[hbm] * 6,
        out_specs=hbm,
        scratch_shapes=[
            pltpu.VMEM(density.shape, jnp.float32),
            pltpu.VMEM(anchor.shape, jnp.float32),
            pltpu.VMEM((4, links), jnp.int32),
            pltpu.VMEM((4, links), jnp.int32),
            pltpu.VMEM(plan.shape, jnp.int32),
            pltpu.SMEM(capacity_levels.shape, jnp.float32),
            pltpu.VMEM(density.shape, jnp.float32),
            pltpu.VMEM((16, all_links), jnp.int32),
            pltpu.VMEM((regions, 8, links), jnp.float32),
            pltpu.VMEM((regions, 8, links), jnp.float32),
            pltpu.VMEM((shares, 16, links), jnp.float32),
            pltpu.VMEM((16, all_links), jnp.float32),
            pltpu.VMEM((all_links, all_links), jnp.bfloat16),
            pltpu.VMEM((16, all_links), jnp.float32),
            pltpu.VMEM((steps, regions * slots, width), jnp.float32),
            pltpu.VMEM((steps, regions * slots, width), jnp.float32),
            pltpu.VMEM((8, all_links), jnp.float32),
            pltpu.VMEM((128, all_links), jnp.float32),
            pltpu.VMEM((links, 128), jnp.float32),
            pltpu.SemaphoreType.DMA((5 + cells,)),
            pltpu.SemaphoreType.DMA((cells,)),
        ]
        + [pltpu.SemaphoreType.DMA((regions,))] * 4
        + [pltpu.SemaphoreType.DMA((shares,))] * 2
        + [pltpu.SemaphoreType.DMA((regions,))] * 2
        + [pltpu.SemaphoreType.DMA((steps, regions))] * 2,
        compiler_params=pltpu.CompilerParams(
            collective_id=0, has_side_effects=True, vmem_limit_bytes=60 * 1024 * 1024
        ),
    )(density, anchor, feeds.T, turns.T, plan, capacity_levels)


def slot_bound(links, regions):
    return 4 * max(1, (links // 2 + 4 * (regions - 2) - 1) // (4 * (regions - 2)))


def local(density, *rest):
    regions = lax.axis_size("region")
    links = density.shape[1]
    shares = lax.axis_size("dest")
    even = regions & (regions - 1) == 0 and shares & (shares - 1) == 0
    if even and regions * links <= 1024 and regions * slot_bound(links, regions) == 128:
        return fused(density, *rest)
    return stepwise(density, *rest)


def solution(mesh):
    in_specs = (
        P(None, ("scen", "region"), "dest"),
        P(("scen", "region"), "dest"),
        P("region", None),
        P("region", None),
        P(None, "region"),
        P(),
    )
    out_specs = P(None, ("scen", "region"), "dest")
    return jax.shard_map(local, mesh=mesh, in_specs=in_specs, out_specs=out_specs, check_vma=False)
```

```python
import functools

import jax
import jax.numpy as jnp
from jax import lax
from jax.experimental import pallas as pl
from jax.experimental.pallas import tpu as pltpu
from jax.sharding import PartitionSpec as P

COMM = 1024


FREE_SPEED = 0.8
WAVE_SPEED = 0.4
JAM_FACTOR = 2.0
EXIT_WEIGHT = 4.0


def one_hot_table(positions, segments):
    return positions[:, None] == jnp.arange(segments, dtype=jnp.int32)[None, :]


def table_total(values, table):
    return jnp.sum(jnp.where(table, values[:, None], 0), axis=0)


def slot_ranks(chosen, owners, peers):
    member = chosen[:, None] & (owners[:, None] == jnp.arange(peers, dtype=jnp.int32)[None, :])
    ranked = jnp.cumsum(member.astype(jnp.int32), axis=0) - 1
    return jnp.sum(jnp.where(member, ranked, 0), axis=1)


def stepwise(density, anchor, feeds, turns, plan, capacity_levels):
    num_cells, num_links, commodity_width = density.shape
    peers = lax.axis_size("region")
    my_region = lax.axis_index("region")
    bucket = 4 * max(1, (num_links // 2 + 4 * (peers - 2) - 1) // (4 * (peers - 2)))
    flat_feed = feeds.reshape(-1)
    flat_turn = turns.reshape(-1)
    is_live = flat_feed >= 0
    owners = jnp.where(is_live, flat_feed // num_links, -1)
    local_ids = jnp.where(is_live, flat_feed % num_links, 0)
    is_remote = is_live & (owners != my_region)
    is_nearby = is_live & (owners == my_region)
    capacity = 2 * bucket
    slots = slot_ranks(is_remote, owners, peers)
    total_slots = peers * capacity
    leader_flat = jnp.where(is_remote, owners * capacity + slots, -1)
    route_flat = jnp.where(is_remote, owners * capacity + slots, -1)
    leader_table = one_hot_table(leader_flat, total_slots)
    route_table = one_hot_table(route_flat, total_slots)
    id_filled = table_total(local_ids, leader_table)
    request_ids = jnp.where(jnp.any(leader_table, axis=0), id_filled, -1).reshape(peers, capacity)
    request_counts = table_total(flat_turn, route_table).reshape(peers, capacity)
    asked_ids, asked_counts = (
        lax.all_to_all(request_ids, "region", split_axis=0, concat_axis=0, tiled=True),
        lax.all_to_all(request_counts, "region", split_axis=0, concat_axis=0, tiled=True),
    )
    flat_asked = asked_ids.reshape(-1)
    nearby_rows = jnp.where(is_nearby, local_ids, -1)
    nearby_table = one_hot_table(nearby_rows, num_links)
    asked_table = one_hot_table(flat_asked, num_links)
    count_total = table_total(jnp.where(is_nearby, flat_turn, 0), nearby_table)
    count_total = count_total + table_total(asked_counts.reshape(-1), asked_table)
    denominator = count_total.astype(jnp.float32) + EXIT_WEIGHT
    gather_ids = jnp.maximum(flat_asked, 0)
    pick_peer = jnp.where(is_remote, owners, 0)
    pick_slot = jnp.where(is_remote, slots, 0)
    live_weight = jnp.where(is_live, flat_turn, 0).astype(jnp.float32)
    level_ids = jnp.arange(capacity_levels.shape[0], dtype=jnp.int32)
    cell_sum, anchor_total = lax.psum((jnp.sum(density, axis=2), jnp.sum(anchor, axis=1)), "dest")
    for step_index in range(plan.shape[0]):
        last_rows = density[num_cells - 1]
        if step_index > 0:
            cell_sum = lax.psum(jnp.sum(density, axis=2), "dest")
        level_match = plan[step_index][:, None] == level_ids[None, :]
        capacity_now = jnp.sum(jnp.where(level_match, capacity_levels[None, :], 0.0), axis=1) * COMM
        sending = jnp.minimum(FREE_SPEED * cell_sum, capacity_now[None, :])
        receiving = jnp.minimum(capacity_now[None, :], WAVE_SPEED * (JAM_FACTOR * COMM - cell_sum))
        per_count = sending[num_cells - 1] / denominator
        unit_share = per_count / cell_sum[num_cells - 1]
        sent_count = per_count[gather_ids].reshape(peers, capacity)
        sent_unit = unit_share[gather_ids].reshape(peers, capacity)
        sent_rows = last_rows[gather_ids].reshape(peers, capacity, commodity_width)
        got_rows, got_count, got_unit = (
            lax.all_to_all(sent_rows, "region", split_axis=0, concat_axis=0, tiled=True),
            lax.all_to_all(sent_count, "region", split_axis=0, concat_axis=0, tiled=True),
            lax.all_to_all(sent_unit, "region", split_axis=0, concat_axis=0, tiled=True),
        )
        pair_count = jnp.where(is_remote, got_count[pick_peer, pick_slot], per_count[local_ids])
        pair_unit = jnp.where(is_remote, got_unit[pick_peer, pick_slot], unit_share[local_ids])
        pair_rows = jnp.where(
            is_remote[:, None], got_rows[pick_peer, pick_slot], last_rows[local_ids]
        )
        demand = jnp.sum((live_weight * pair_count).reshape(num_links, 4), axis=1) + anchor_total
        ratio = receiving[0] / jnp.maximum(receiving[0], demand)
        mixing = (live_weight * pair_unit).reshape(num_links, 4)
        gathered = jnp.sum(
            mixing[:, :, None] * pair_rows.reshape(num_links, 4, commodity_width), axis=1
        )
        inflow = ratio[:, None] * (gathered + anchor)
        granted = (live_weight.reshape(num_links, 4) * ratio[:, None]).reshape(-1)
        send_back = table_total(granted, route_table).reshape(peers, capacity)
        returned = lax.all_to_all(send_back, "region", split_axis=0, concat_axis=0, tiled=True)
        passed = table_total(jnp.where(is_nearby, granted, 0.0), nearby_table)
        passed = passed + table_total(returned.reshape(-1), asked_table)
        outflow = (unit_share * (passed + EXIT_WEIGHT))[:, None] * last_rows
        through = jnp.minimum(sending[:-1], receiving[1:])
        moving = (through / cell_sum[:-1])[:, :, None] * density[:-1]
        density = (
            density
            - jnp.pad(moving, ((0, 1), (0, 0), (0, 0)))
            + jnp.pad(moving, ((1, 0), (0, 0), (0, 0)))
        )
        density = jnp.concatenate(
            [
                density[:1] + inflow[None],
                density[1 : num_cells - 1],
                density[num_cells - 1 :] - outflow[None],
            ],
            axis=0,
        )
    return density


def split_two(values):
    high = values.astype(jnp.bfloat16)
    low = (values - high.astype(jnp.float32)).astype(jnp.bfloat16)
    return high, low


def dot(a, b, dims):
    return lax.dot_general(a, b, (dims, ((), ())), preferred_element_type=jnp.float32)


NN = ((1,), (0,))
NT = ((1,), (1,))


def vector_dot(row, matrix, dims):
    first = row.astype(jnp.bfloat16).astype(jnp.float32)
    second = (row - first).astype(jnp.bfloat16).astype(jnp.float32)
    third = row - first - second
    at = lax.broadcasted_iota(jnp.int32, (16, row.shape[1]), 0)
    stacked = jnp.where(at == 0, first, jnp.where(at == 1, second, jnp.where(at == 2, third, 0.0)))
    return jnp.sum(dot(stacked.astype(jnp.bfloat16), matrix, dims), axis=0, keepdims=True)


def across(index, mask):
    bit = 1
    while bit <= mask:
        if mask & bit:
            index = index + bit - 2 * bit * lax.rem(index // bit, 2)
        bit *= 2
    return index


def network_kernel(
    regions, shares, slots, steps,
    density_hbm, anchor_hbm, feeds_hbm, turns_hbm, plan_hbm, levels_hbm, out_ref,
    density_ref, anchor_ref, feeds_ref, turns_ref, plan_ref, levels_ref,
    ints_all, asking, asked, parts, totals, matrix, keys, rows_out, rows_in, weights, coefs, columns,
    in_sem, int_send, int_recv, key_send, key_recv, part_send, part_recv, total_send, total_recv, row_send, row_recv,
):
    cells, links, width = density_ref.shape
    all_links = regions * links
    held = regions * slots
    me = lax.axis_index("region")
    share = lax.axis_index("dest")

    def lanes(region):
        return pl.ds(pl.multiple_of(region * links, links), links)

    def slot_rows(region):
        return pl.ds(pl.multiple_of(region * slots, slots), slots)

    mine = lanes(me)

    def start_all(copies):
        for copy in copies:
            copy.start()
        return copies

    def wait_all(copies):
        for copy in copies:
            copy.wait()

    def to_region(src, dst, send, recv, mask):
        return pltpu.make_async_remote_copy(
            src_ref=src, dst_ref=dst, send_sem=send.at[mask], recv_sem=recv.at[mask],
            device_id={"region": across(me, mask)}, device_id_type=pl.DeviceIdType.MESH,
        )

    masks = list(range(regions // 2, regions)) + list(range(regions // 2 - 1, 0, -1))

    barrier = pltpu.get_barrier_semaphore()
    for mask in masks:
        pl.semaphore_signal(barrier, inc=1, device_id={"region": across(me, mask)}, device_id_type=pl.DeviceIdType.MESH)
    for mask in range(1, shares):
        pl.semaphore_signal(barrier, inc=1, device_id={"dest": across(share, mask)}, device_id_type=pl.DeviceIdType.MESH)

    small = start_all([
        pltpu.make_async_copy(src, dst, in_sem.at[at]) for at, (src, dst) in enumerate(
            [(feeds_hbm, feeds_ref), (turns_hbm, turns_ref), (plan_hbm, plan_ref), (levels_hbm, levels_ref)])
    ])
    anchor_copy = pltpu.make_async_copy(anchor_hbm, anchor_ref, in_sem.at[4])
    cell_copies = {
        cell: pltpu.make_async_copy(density_hbm.at[cell], density_ref.at[cell], in_sem.at[5 + cell])
        for cell in range(cells - 1, -1, -1)
    }
    start_all(list(cell_copies.values()) + [anchor_copy])
    rows_in[:, slot_rows(me), :] = jnp.zeros((steps, slots, width), jnp.float32)
    asked[me] = jnp.full((8, links), -1.0, jnp.float32)
    coefs[...] = jnp.zeros_like(coefs)
    wait_all(small)

    def counts_of(feeds, turns):
        named = lax.broadcasted_iota(jnp.int32, (all_links, links), 0)
        count = jnp.zeros((all_links, links), jnp.float32)
        for entry in range(4):
            count = count + jnp.where(
                feeds[entry : entry + 1] == named, turns[entry : entry + 1].astype(jnp.float32), 0.0
            )
        return count.astype(jnp.bfloat16)

    ints_all[0:4, mine] = feeds_ref[...]
    ints_all[4:8, mine] = turns_ref[...]
    ints_all[8 : 8 + steps, mine] = plan_ref[...]
    own_counts = counts_of(feeds_ref[...], turns_ref[...])
    matrix[:, mine] = own_counts
    named_at = jnp.where(dot(jnp.ones((16, links), jnp.bfloat16), own_counts, NT) > 0.0, 1.0, 0.0)
    before = lax.broadcasted_iota(jnp.int32, (links, links), 0) < lax.broadcasted_iota(jnp.int32, (links, links), 1)
    before = jnp.where(before, 1.0, 0.0).astype(jnp.bfloat16)
    for block in range(regions):
        at = slice(block * links, (block + 1) * links)
        rank = dot(named_at[:, at].astype(jnp.bfloat16), before, NN)
        key = jnp.where(named_at[:, at] > 0.0, rank, -1.0)
        keys[:, at] = key
        asking[block] = key[0:8]

    pl.semaphore_wait(barrier, regions + shares - 2)
    key_copies = start_all([
        to_region(asking.at[across(me, mask)], asked.at[me], key_send, key_recv, mask) for mask in masks
    ])
    int_copies = start_all([
        to_region(ints_all.at[:, mine], ints_all.at[:, mine], int_send, int_recv, mask) for mask in masks
    ])

    summed = jnp.zeros((16, links), jnp.float32)
    pick = lax.broadcasted_iota(jnp.int32, (16, width), 0)
    for cell in list(cell_copies) + [cells]:
        if cell < cells:
            cell_copies[cell].wait()
        else:
            anchor_copy.wait()
        high, low = split_two(density_ref[cell] if cell < cells else anchor_ref[...])
        ones = jnp.where(pick == cell, 1.0, 0.0).astype(jnp.bfloat16)
        summed = summed + dot(ones, high, NT) + dot(ones, low, NT)
    parts[share] = summed

    part_copies = start_all([
        pltpu.make_async_remote_copy(
            src_ref=parts.at[share], dst_ref=parts.at[share],
            send_sem=part_send.at[mask], recv_sem=part_recv.at[mask],
            device_id={"dest": across(share, mask)}, device_id_type=pl.DeviceIdType.MESH,
        )
        for mask in range(1, shares)
    ])

    wait_all(key_copies)
    slot_at = lax.broadcasted_iota(jnp.int32, (slots, links), 0).astype(jnp.float32)
    chosen = jnp.concatenate(
        [jnp.where(asked[region, 0:1, :] == slot_at, 1.0, 0.0) for region in range(regions)], axis=0
    ).astype(jnp.bfloat16)
    row_copies = []
    for back in range(steps):
        high, low = split_two(density_ref[cells - 1 - back])
        rows_out[back] = dot(chosen, high, NN) + dot(chosen, low, NN)
        row_copies.append(start_all([
            to_region(
                rows_out.at[back, slot_rows(across(me, mask)), :], rows_in.at[back, slot_rows(me), :],
                row_send.at[back], row_recv.at[back], mask,
            )
            for mask in masks
        ]))
        if back == 0:
            wait_all(part_copies)
            total_here = parts[0]
            for other in range(1, shares):
                total_here = total_here + parts[other]
            totals[:, mine] = total_here
            total_copies = start_all([
                to_region(totals.at[:, mine], totals.at[:, mine], total_send, total_recv, mask) for mask in masks
            ])

    lane = lax.broadcasted_iota(jnp.int32, (1, all_links), 1)
    wanted = keys[0:1, :]
    wanted = jnp.where(
        (wanted >= 0.0) & (lane // links != me), wanted + (lane // links * slots).astype(jnp.float32), -1.0
    )
    held_at = jnp.where(
        lax.broadcasted_iota(jnp.int32, (held, all_links), 0).astype(jnp.float32) == wanted, 1.0, 0.0
    ).astype(jnp.bfloat16)
    far_counts = jnp.transpose(dot(held_at, own_counts, NN))
    near_counts = jnp.transpose(matrix[mine, mine].astype(jnp.float32))

    wait_all(int_copies)
    for mask in masks:
        theirs = lanes(across(me, mask))
        matrix[:, theirs] = counts_of(ints_all[0:4, theirs], ints_all[4:8, theirs])
    denominator = dot(jnp.ones((16, all_links), jnp.bfloat16), matrix[...], NT)[0:1] + EXIT_WEIGHT

    wait_all(total_copies)
    cell_row = lax.broadcasted_iota(jnp.int32, (cells, all_links), 0)

    def moved_up(values):
        return jnp.where(cell_row == 0, 0.0, pltpu.roll(values, 1, 0))

    total = totals[0:cells, :]
    anchor_total = totals[cells : cells + 1, :]
    kept = [jnp.ones((cells, all_links), jnp.float32)]
    entered = []
    weight_rows = []
    for step in range(steps):
        plan_row = ints_all[8 + step : 9 + step, :]
        capacity = jnp.zeros((1, all_links), jnp.float32)
        for level in range(levels_ref.shape[0]):
            capacity = jnp.where(plan_row == level, levels_ref[level], capacity)
        capacity = capacity * COMM
        sending = jnp.minimum(FREE_SPEED * total, capacity)
        receiving = jnp.minimum(capacity, WAVE_SPEED * (JAM_FACTOR * COMM - total))
        per_count = sending[cells - 1 : cells] / denominator
        unit_share = per_count / total[cells - 1 : cells]
        demand = vector_dot(per_count, matrix[...], NN) + anchor_total
        ratio = receiving[0:1] / jnp.maximum(receiving[0:1], demand)
        passed = vector_dot(ratio, matrix[...], NT)
        leaving = unit_share * (passed + EXIT_WEIGHT)
        through = jnp.where(cell_row < cells - 1, jnp.minimum(sending, pltpu.roll(receiving, cells - 1, 0)), 0.0)
        going = through / total
        staying = 1.0 - going - jnp.where(cell_row == cells - 1, leaving, 0.0)
        weight_rows += [unit_share * part[cells - 1 : cells] for part in kept]
        total = (
            total - through + moved_up(through)
            + jnp.where(cell_row == 0, ratio * demand, 0.0)
            - jnp.where(cell_row == cells - 1, leaving * total, 0.0)
        )
        zero = jnp.zeros((cells, all_links), jnp.float32)
        kept = [
            staying * same + moved_up(going * above) for same, above in zip(kept + [zero], [zero] + kept)
        ]
        entered = [staying * part + moved_up(going * part) for part in entered]
        entered.append(jnp.where(cell_row == 0, ratio, 0.0))

    for index, row in enumerate(weight_rows):
        weights[index : index + 1, :] = row
    blocks = kept + entered + [functools.reduce(lambda a, b: a + b, entered)]
    for index, block in enumerate(blocks):
        coefs[index * cells : (index + 1) * cells, :] = block
    columns[...] = jnp.transpose(coefs[:, mine])

    def column(block, cell):
        at = block * cells + cell
        return columns[:, at : at + 1]

    weight_high, weight_low = split_two(weights[...])
    far_weights = dot(weight_high, held_at, NT) + dot(weight_low, held_at, NT)
    near_weights = weights[:, mine]

    def mixing(counts, row_weights, back):
        pieces = []
        for cell in range(steps - back):
            piece = None
            for step in range(back, steps - cell):
                index = step * (step + 1) // 2 + back
                term = column(steps + 1 + step, cell) * row_weights[index : index + 1]
                piece = term if piece is None else piece + term
            pieces.append(counts * piece)
        return split_two(jnp.concatenate(pieces, axis=0))

    def mixed(mixing_pair, content):
        high, low = mixing_pair
        content_high, content_low = split_two(content)
        return dot(high, content_high, NN) + dot(low, content_high, NN) + dot(high, content_low, NN)

    far_mixing = [mixing(far_counts, far_weights, back) for back in range(steps)]
    near = [
        mixed(mixing(near_counts, near_weights, back), density_ref[cells - 1 - back]) for back in range(steps)
    ]
    for cell in range(cells):
        value = column(0, cell) * density_ref[cell]
        for back in range(1, min(steps, cell) + 1):
            value = value + column(back, cell) * density_ref[cell - back]
        if cell < steps:
            value = value + column(2 * steps + 1, cell) * anchor_ref[...]
            for back in range(steps - cell):
                value = value + near[back][cell * links : (cell + 1) * links]
        out_ref[cell] = value

    for back in range(steps):
        wait_all(row_copies[back])
        far = mixed(far_mixing[back], rows_in[back])
        for cell in range(steps - back):
            out_ref[cell] = out_ref[cell] + far[cell * links : (cell + 1) * links]


def fused(density, anchor, feeds, turns, plan, capacity_levels):
    cells, links, width = density.shape
    steps = plan.shape[0]
    regions = lax.axis_size("region")
    shares = lax.axis_size("dest")
    slots = slot_bound(links, regions)
    all_links = regions * links
    hbm = pl.BlockSpec(memory_space=pltpu.HBM)
    return pl.pallas_call(
        functools.partial(network_kernel, regions, shares, slots, steps),
        out_shape=jax.ShapeDtypeStruct(density.shape, jnp.float32),
        in_specs=[hbm] * 6,
        out_specs=pl.BlockSpec(memory_space=pltpu.VMEM),
        scratch_shapes=[
            pltpu.VMEM(density.shape, jnp.float32),
            pltpu.VMEM(anchor.shape, jnp.float32),
            pltpu.VMEM((4, links), jnp.int32),
            pltpu.VMEM((4, links), jnp.int32),
            pltpu.VMEM(plan.shape, jnp.int32),
            pltpu.SMEM(capacity_levels.shape, jnp.float32),
            pltpu.VMEM((16, all_links), jnp.int32),
            pltpu.VMEM((regions, 8, links), jnp.float32),
            pltpu.VMEM((regions, 8, links), jnp.float32),
            pltpu.VMEM((shares, 16, links), jnp.float32),
            pltpu.VMEM((16, all_links), jnp.float32),
            pltpu.VMEM((all_links, all_links), jnp.bfloat16),
            pltpu.VMEM((16, all_links), jnp.float32),
            pltpu.VMEM((steps, regions * slots, width), jnp.float32),
            pltpu.VMEM((steps, regions * slots, width), jnp.float32),
            pltpu.VMEM((8, all_links), jnp.float32),
            pltpu.VMEM((128, all_links), jnp.float32),
            pltpu.VMEM((links, 128), jnp.float32),
            pltpu.SemaphoreType.DMA((5 + cells,)),
        ]
        + [pltpu.SemaphoreType.DMA((regions,))] * 4
        + [pltpu.SemaphoreType.DMA((shares,))] * 2
        + [pltpu.SemaphoreType.DMA((regions,))] * 2
        + [pltpu.SemaphoreType.DMA((steps, regions))] * 2,
        compiler_params=pltpu.CompilerParams(
            collective_id=0, has_side_effects=True, vmem_limit_bytes=32 * 1024 * 1024
        ),
    )(*(pltpu.with_memory_space_constraint(x, pltpu.HBM) for x in (density, anchor, feeds.T, turns.T, plan, capacity_levels)))


def slot_bound(links, regions):
    return 4 * max(1, (links // 2 + 4 * (regions - 2) - 1) // (4 * (regions - 2)))


def local(density, *rest):
    regions = lax.axis_size("region")
    links = density.shape[1]
    shares = lax.axis_size("dest")
    even = regions & (regions - 1) == 0 and shares & (shares - 1) == 0
    if even and regions * links <= 1024 and regions * slot_bound(links, regions) == 128:
        return fused(density, *rest)
    return stepwise(density, *rest)


def solution(mesh):
    in_specs = (
        P(None, ("scen", "region"), "dest"),
        P(("scen", "region"), "dest"),
        P("region", None),
        P("region", None),
        P(None, "region"),
        P(),
    )
    out_specs = P(None, ("scen", "region"), "dest")
    return jax.shard_map(local, mesh=mesh, in_specs=in_specs, out_specs=out_specs, check_vma=False)
```
